256 devices in a mesh: rows: 64 (over x, z, y_lo), strips: 4 (over y_hi, core).
Axes of the slice: x: 4, y: 4 (y_hi: 2, y_lo: 2; y = y_hi * 2 + y_lo), z: 8, core: 2. Of those that a mesh axis runs over, the one named last changes fastest.
Arguments:
- tokens: bfloat16 [64, 24, 64, 1280], P('rows', None, 'strips'), may hold values from -8 to 8
- stale_kv: bfloat16 [64, 2, 1536, 1280], P('rows', None, 'strips'), may hold values from -180 to 180
- stale_moments: float32 [64, 4, 2, 32], P('rows', 'strips'), as said below
- norm_gain: float32 [1280], replicated, may hold values from 0.1 to 1.9
- norm_bias: float32 [1280], replicated, may hold values from -3 to 3
- w_query: bfloat16 [1280, 1280], P('rows'), may hold values from -0.33398438 to 0.33398438
- w_key: bfloat16 [1280, 1280], P('rows'), may hold values from -0.1953125 to 0.1953125
- w_value: bfloat16 [1280, 1280], P('rows'), may hold values from -0.15625 to 0.15625
- w_out: bfloat16 [1280, 1280], P('rows'), may hold values from -0.33398438 to 0.33398438
Outputs:
- attended: bfloat16 [64, 24, 64, 1280], P('rows', None, 'strips')
- fresh_kv: bfloat16 [64, 2, 1536, 1280], P('rows', None, 'strips')
- fresh_sums: float32 [64, 4, 32], P('rows', 'strips')
- fresh_squares: float32 [64, 4, 32], P('rows', 'strips')
The draws below stay inside these ranges and needn't reach their ends.
Inputs may be any that keep to these rules, and one draw needn't show every extreme that they name: `stale_moments`: each strip's entries are a sum of 15360 values and the sum of their squares.
All inputs are finite; a program needn't handle non-finite values.
Results may differ from the reference program's by a relative error of at most 0.0075.
The reference program's roundings to bfloat16 on the way (of `normed` and `heads_out`) count: a program that leaves them out, or rounds other values in their place, can miss the bound.
Values may be sent and summed in bfloat16 or wider, within the bound.
A program may use at most 128 MiB of HBM per device.

```python
import jax
import jax.numpy as jnp
from jax import lax

C = 1280
GROUPS = 32
HEADS = 20
HEAD = 64
ROWS_IMG = 24
SW = 16
CG = 40
HD = 1280
TOK_DEV = 384
GRID_COLS = 64
KEYS = 1536
IMAGES = 64
N_STRIPS = 4


def draw_stale_kv(key, part):
    first = jax.random.fold_in(key, 0)
    base = jnp.clip(jax.random.normal(first, (IMAGES, 2, KEYS, HD), jnp.float32), -6.0, 6.0)
    return base.astype(jnp.bfloat16)


def draw_stale_moments(key, part):
    first, second = jax.random.split(key)
    count = float(TOK_DEV * CG)
    index = jnp.arange(N_STRIPS, dtype=jnp.float32)[None, :, None]
    rising = 1.0 + 2.0 * index / max(N_STRIPS - 1, 1)
    mean = 0.3 * jax.random.normal(first, (IMAGES, N_STRIPS, GROUPS), jnp.float32)
    var = jnp.exp(jax.random.uniform(second, (IMAGES, N_STRIPS, GROUPS), jnp.float32, -0.5, 0.35)) * rising
    return jnp.stack([count * mean, count * (var + mean * mean)], axis=2).astype(jnp.float32)


def shard_levels(stream_key, extent, pieces, least, largest):
    factor_of = 1.0
    for axis_at, parts in pieces:
        heights = jax.random.uniform(jax.random.fold_in(jax.random.fold_in(stream_key, 6), axis_at), (parts,), jnp.float32, least / len(pieces), largest / len(pieces))
        factor_of = factor_of * jnp.repeat(jnp.exp(heights), extent[axis_at] // parts).reshape((-1,) + (1,) * (len(extent) - 1 - axis_at))
    return factor_of


def normal_values(stream_key, shape, deviation, limit, pieces=(), kind=jnp.bfloat16):
    factor_of = shard_levels(stream_key, shape, pieces, -0.22, 0.18) if pieces else 1.0
    entries = jax.random.normal(stream_key, shape, jnp.float32) * deviation * factor_of
    return jnp.minimum(jnp.maximum(entries, -limit), limit).astype(kind)


def setup_inputs(seed: int = 0) -> dict:
    keys = jax.random.split(jax.random.key(seed), 10)
    tokens = normal_values(keys[0], (IMAGES, ROWS_IMG, GRID_COLS, C), 1.3, 8.0, ((0, 64), (2, 4)))
    stale_kv = draw_stale_kv(jax.random.fold_in(keys[9], 71), 0)
    stale_moments = draw_stale_moments(jax.random.fold_in(keys[9], 71), 0)
    norm_gain = jnp.clip(1.0 + 0.18 * jax.random.normal(keys[3], (C,), jnp.float32), 0.1, 1.9)
    norm_bias = normal_values(keys[4], (C,), 0.5, 3.0, (), jnp.float32)
    w_query = normal_values(keys[5], (C, HD), (2.0 / C ** 0.5), 0.33398438, ((0, 64),))
    w_key = normal_values(keys[6], (C, HD), (1.15 / C ** 0.5), 0.1953125, ((0, 64),))
    w_value = normal_values(keys[7], (C, HD), C ** -0.5, 0.15625, ((0, 64),))
    w_out = normal_values(keys[8], (HD, C), (2.0 / HD ** 0.5), 0.33398438, ((0, 64),))
    return dict(tokens=tokens, stale_kv=stale_kv, stale_moments=stale_moments, norm_gain=norm_gain, norm_bias=norm_bias, w_query=w_query, w_key=w_key, w_value=w_value, w_out=w_out)


def reference(tokens, stale_kv, stale_moments, norm_gain, norm_bias, w_query, w_key, w_value, w_out):
    count = float(KEYS * CG)
    positions = jnp.arange(KEYS, dtype=jnp.int32)
    highest = lax.Precision.HIGHEST

    def one_image(items):
        image, kv_old, moments_old = items
        blocks = image.reshape(ROWS_IMG, N_STRIPS, SW, C).transpose(1, 0, 2, 3).reshape(N_STRIPS, TOK_DEV, C).astype(jnp.float32)
        grouped = blocks.reshape(N_STRIPS, TOK_DEV, GROUPS, CG)
        fresh = jnp.stack([grouped.sum(axis=(1, 3)), (grouped * grouped).sum(axis=(1, 3))], axis=1)
        mixed = lax.optimization_barrier(jnp.sum(moments_old, axis=0))[None] - moments_old + fresh
        mean = mixed[:, 0] / count
        var = mixed[:, 1] / count - mean * mean
        rstd = lax.rsqrt(var + 1e-05)
        normed = ((grouped - mean[:, None, :, None]) * rstd[:, None, :, None]).reshape(N_STRIPS, TOK_DEV, C)
        normed = (normed * norm_gain + norm_bias).astype(jnp.bfloat16).reshape(KEYS, C)
        query = (jnp.dot(normed, w_query, preferred_element_type=jnp.float32) * (1.0 / HEAD ** 0.5)).astype(jnp.bfloat16)
        key = jnp.dot(normed, w_key, preferred_element_type=jnp.float32).astype(jnp.bfloat16)
        value = jnp.dot(normed, w_value, preferred_element_type=jnp.float32).astype(jnp.bfloat16)
        far_keys = kv_old[0].astype(jnp.float32).reshape(KEYS, HEADS, HEAD)
        far_vals = kv_old[1].astype(jnp.float32).reshape(KEYS, HEADS, HEAD)

        def one_strip(strip):
            start = (strip * TOK_DEV).astype(jnp.int32)
            qry = lax.dynamic_slice_in_dim(query, start, TOK_DEV, 0).astype(jnp.float32).reshape(TOK_DEV, HEADS, HEAD)
            near_k = lax.dynamic_slice_in_dim(key, start, TOK_DEV, 0).astype(jnp.float32).reshape(TOK_DEV, HEADS, HEAD)
            near_v = lax.dynamic_slice_in_dim(value, start, TOK_DEV, 0).astype(jnp.float32).reshape(TOK_DEV, HEADS, HEAD)
            far_s = jnp.einsum('qhe,khe->hqk', qry, far_keys, precision=highest)
            inside = (positions >= start) & (positions < start + TOK_DEV)
            far_s = jnp.where(inside[None, None, :], jnp.float32(-1e+30), far_s)
            near_s = jnp.einsum('qhe,khe->hqk', qry, near_k, precision=highest)
            top = jnp.maximum(far_s.max(axis=-1), near_s.max(axis=-1))
            far_p = jnp.exp(far_s - top[..., None])
            near_p = jnp.exp(near_s - top[..., None])
            total = far_p.sum(axis=-1) + near_p.sum(axis=-1)
            weighted = jnp.einsum('hqk,khe->hqe', far_p, far_vals, precision=highest) + jnp.einsum('hqk,khe->hqe', near_p, near_v, precision=highest)
            heads_out = (weighted / total[..., None]).transpose(1, 0, 2).reshape(TOK_DEV, HD).astype(jnp.bfloat16)
            return jnp.dot(heads_out, w_out, preferred_element_type=jnp.float32).astype(jnp.bfloat16)
        outs = lax.map(one_strip, jnp.arange(N_STRIPS, dtype=jnp.int32))
        attended = outs.reshape(N_STRIPS, ROWS_IMG, SW, C).transpose(1, 0, 2, 3).reshape(ROWS_IMG, GRID_COLS, C)
        return (attended, jnp.stack([key, value]), fresh[:, 0], fresh[:, 1])
    attended, fresh_kv, fresh_sums, fresh_squares = lax.map(one_image, (tokens, stale_kv, stale_moments))
    return (attended, fresh_kv, fresh_sums, fresh_squares)
```

```python
import jax
import jax.numpy as jnp
from jax import lax
from jax.experimental import pallas as pl
from jax.experimental.pallas import tpu as pltpu
from jax.sharding import PartitionSpec as P

MESH = pl.DeviceIdType.MESH
F32 = jnp.float32
BF16 = jnp.bfloat16

TOK = 384
CH = 1280
HALF = 640
LANES = 128
WAVES = 5
NX, NZ, NY = 4, 8, 2
SHARD = 20
GROUPS = 32
PER_GROUP = 40


def dot(a, b, dims=((1,), (0,)), precision=None):
    return lax.dot_general(a, b, (dims, ((), ())), precision=precision, preferred_element_type=F32)


def kernel(
    tok_ref, kv_ref, mom_ref, gain_ref, bias_ref, wq_ref, wk_ref, wv_ref, wo_ref,
    att_ref, fkv_ref, fs_ref, fq_ref,
    w_buf, wo_buf, w_nat, wo_nat, pick_a, pick_b, tail, kvb, nrm, qb, ho, ho_out, moms,
    y_s, y_r, z_s, z_r, x_s, x_r, xx_s, xx_r, zo_s, zo_r, xo_s, xo_r, xxo_s, xxo_r,
    kv_s, kv_r, kv_l, mom_s, mom_r, nrm_s, nrm_r, fkv_s, fkv_r, fkv_l, ho_s, ho_r, won_s, won_r,
):
    row = lax.axis_index("rows")
    strip = lax.axis_index("strips")
    ylo = row % 2
    z = (row // 2) % NZ
    x = row // (2 * NZ)
    core = strip % 2
    yhi = strip // 2

    sib = (row, yhi * 2 + 1 - core)
    far = (row, (1 - yhi) * 2 + core)
    far_other = (row, (1 - yhi) * 2 + 1 - core)
    y_peer = (x * 16 + z * 2 + 1 - ylo, strip)
    z_peers = [(x * 16 + ((z + d) % NZ) * 2 + ylo, strip) for d in range(1, NZ)]
    xl = (x + NX - 1) % NX
    xr = (x + 1) % NX
    x_far = (x + 2) % NX
    x_left = (xl * 16 + z * 2 + ylo, strip)
    x_right = (xr * 16 + z * 2 + ylo, strip)

    barrier = pltpu.get_barrier_semaphore()
    everyone = [sib, far, far_other, y_peer, x_left, x_right] + z_peers
    for peer in everyone:
        pl.semaphore_signal(barrier, inc=1, device_id=peer, device_id_type=MESH)

    def remote(src, dst, send, recv, to):
        return pltpu.make_async_remote_copy(
            src_ref=src, dst_ref=dst, send_sem=send, recv_sem=recv, device_id=to, device_id_type=MESH
        )

    mine = pl.ds(pl.multiple_of(core * HALF, LANES), HALF)
    for t, ref in enumerate((wq_ref, wk_ref, wv_ref, wo_ref)):
        rows = ref[:, mine]
        for g in range(WAVES):
            piece = rows[:16, g * LANES : (g + 1) * LANES]
            if t < 3:
                w_buf[g, x, z, ylo, t] = piece
            else:
                wo_buf[x, z, ylo, g] = piece
        tail[4 * t : 4 * t + 4, :] = rows.astype(F32)[16:SHARD, :]
    rest = tail[...].astype(BF16)
    for g in range(WAVES):
        w_buf[g, x, z, ylo, 3] = rest[:, g * LANES : (g + 1) * LANES]
    moms[0] = jnp.zeros((8, LANES), F32)
    moms[0, 0:2, 0:GROUPS] = mom_ref[...]

    pl.semaphore_wait(barrier, len(everyone))

    def y_copies():
        here = w_buf.at[:, x, z, ylo]
        ohere = wo_buf.at[x, z, ylo]
        return [
            remote(here, here, y_s.at[0], y_r.at[0], y_peer),
            remote(ohere, ohere, y_s.at[1], y_r.at[1], y_peer),
        ]

    def y_wait():
        there = w_buf.at[:, x, z, 1 - ylo]
        othere = wo_buf.at[x, z, 1 - ylo]
        remote(there, there, y_s.at[0], y_r.at[0], y_peer).wait_recv()
        remote(othere, othere, y_s.at[1], y_r.at[1], y_peer).wait_recv()

    def z_copies(g):
        return [
            remote(w_buf.at[g, x, z], w_buf.at[g, x, z], z_s.at[g, d], z_r.at[g, d], z_peers[d])
            for d in range(NZ - 1)
        ]

    def z_wait(g):
        for d in range(NZ - 1):
            there = w_buf.at[g, x, (z + NZ - 1 - d) % NZ]
            remote(there, there, z_s.at[g, d], z_r.at[g, d], z_peers[d]).wait_recv()

    def zo_copies():
        return [
            remote(wo_buf.at[x, z], wo_buf.at[x, z], zo_s.at[d], zo_r.at[d], z_peers[d])
            for d in range(NZ - 1)
        ]

    def zo_wait():
        for d in range(NZ - 1):
            there = wo_buf.at[x, (z + NZ - 1 - d) % NZ]
            remote(there, there, zo_s.at[d], zo_r.at[d], z_peers[d]).wait_recv()

    def x_copies(buf, send, recv):
        here = buf(x, 0, NZ)
        return [
            remote(here, here, send(0), recv(0), x_right),
            remote(here, here, send(1), recv(1), x_left),
        ]

    def x_wait(buf, send, recv):
        for i, at in ((0, xl), (1, xr)):
            there = buf(at, 0, NZ)
            remote(there, there, send(i), recv(i), x_right).wait_recv()

    def xx_copies(buf, send, recv):
        first, second = buf(xl, 0, NZ // 2), buf(xr, NZ // 2, NZ // 2)
        return [
            remote(first, first, send(0), recv(0), x_right),
            remote(second, second, send(1), recv(1), x_left),
        ]

    def xx_wait(buf, send, recv):
        for i in (0, 1):
            there = buf(x_far, i * (NZ // 2), NZ // 2)
            remote(there, there, send(i), recv(i), x_right).wait_recv()

    def wave(g, send, recv):
        return (
            lambda at, first, count: w_buf.at[g, at, pl.ds(first, count)],
            lambda i: send.at[g, i],
            lambda i: recv.at[g, i],
        )

    def owave(send, recv):
        return (
            lambda at, first, count: wo_buf.at[at, pl.ds(first, count)],
            lambda i: send.at[i],
            lambda i: recv.at[i],
        )

    def lanes(which, g):
        return pl.ds(pl.multiple_of(which * HALF + g * LANES, LANES), LANES)

    def block(i):
        return pl.ds(i * TOK, TOK)

    def kv_copies(g):
        mine_g, other_g = kv_ref.at[:, :, lanes(core, g)], kv_ref.at[:, :, lanes(1 - core, g)]
        return [
            remote(other_g, kvb.at[g, :, block(0)], kv_s.at[g, 0], kv_r.at[g, 0], sib),
            remote(mine_g, kvb.at[g, :, block(2)], kv_s.at[g, 1], kv_r.at[g, 1], far),
            remote(other_g, kvb.at[g, :, block(3)], kv_s.at[g, 2], kv_r.at[g, 2], far_other),
        ]

    def kv_own(g):
        return pltpu.make_async_copy(kv_ref.at[:, :, lanes(core, g)], kvb.at[g, :, block(5)], kv_l.at[g])

    def kv_wait(g):
        for i, b in enumerate((0, 2, 3)):
            there = kvb.at[g, :, block(b)]
            remote(there, there, kv_s.at[g, i], kv_r.at[g, i], sib).wait_recv()
        kv_own(g).wait()

    def mom_copies():
        return [
            remote(moms.at[0], moms.at[i + 1], mom_s.at[i], mom_r.at[i], to)
            for i, to in enumerate((sib, far, far_other))
        ]

    def nrm_copy():
        return remote(nrm.at[pl.ds(0, TOK)], nrm.at[pl.ds(TOK, TOK)], nrm_s, nrm_r, sib)

    def fkv_copy(g):
        return remote(kvb.at[g, :, block(4)], fkv_ref.at[:, :, lanes(core, g)], fkv_s.at[g], fkv_r.at[g], sib)

    def fkv_own(g):
        return pltpu.make_async_copy(kvb.at[g, :, block(1)], fkv_ref.at[:, :, lanes(core, g)], fkv_l.at[g])

    def fkv_wait(g):
        there = fkv_ref.at[:, :, lanes(1 - core, g)]
        remote(there, there, fkv_s.at[g], fkv_r.at[g], sib).wait_recv()

    def ho_copy(g):
        return remote(ho_out.at[g], ho.at[core * WAVES + g], ho_s.at[g], ho_r.at[g], sib)

    def ho_wait(g):
        there = ho.at[(1 - core) * WAVES + g]
        remote(there, there, ho_s.at[g], ho_r.at[g], sib).wait_recv()

    def won_copy():
        return remote(wo_nat.at[core], wo_nat.at[core], won_s, won_r, sib)

    def start(copies):
        for copy in copies:
            copy.start()

    start(mom_copies())
    start(y_copies())
    start(kv_copies(0))
    kv_own(0).start()
    start(kv_copies(1))
    kv_own(1).start()

    channel = lax.broadcasted_iota(jnp.int32, (CH, LANES), 0)
    group = lax.broadcasted_iota(jnp.int32, (CH, LANES), 1)
    member = jnp.where((channel >= group * PER_GROUP) & (channel < (group + 1) * PER_GROUP), 1.0, 0.0)
    toks = tok_ref[...].astype(F32)
    sums = jnp.sum(toks, axis=0, keepdims=True)
    squares = jnp.sum(toks * toks, axis=0, keepdims=True)
    pick = lax.broadcasted_iota(jnp.int32, (8, CH), 0)
    stacked = jnp.where(pick == 0, sums, jnp.where(pick == 1, squares, 0.0))
    fresh = dot(stacked, member, precision=lax.Precision.HIGHEST)
    fs_ref[...] = fresh[0:1, 0:GROUPS]
    fq_ref[...] = fresh[1:2, 0:GROUPS]

    y_wait()
    start(z_copies(0))
    start(z_copies(1))

    k_at = lax.broadcasted_iota(jnp.int32, (320, 256), 0)
    j_at = lax.broadcasted_iota(jnp.int32, (320, 256), 1)
    base = (j_at >> 4) * SHARD
    pick_a[...] = jnp.where(k_at == base + (j_at & 15), 1.0, 0.0).astype(BF16)
    for t in range(4):
        hit = (k_at == base + 16 + (j_at & 3)) & (((j_at >> 2) & 3) == t)
        pick_b[t] = jnp.where(hit, 1.0, 0.0).astype(BF16)

    for i in range(3):
        there = moms.at[i + 1]
        remote(there, there, mom_s.at[i], mom_r.at[i], sib).wait_recv()
    mixed = (moms[1] + moms[2] + moms[3]) + fresh
    count = float(TOK * 4 * PER_GROUP)
    mean = mixed[0:1, :] / count
    var = mixed[1:2, :] / count - mean * mean
    rstd = lax.rsqrt(var + 1e-05)
    pick = lax.broadcasted_iota(jnp.int32, (8, LANES), 0)
    inside = lax.broadcasted_iota(jnp.int32, (8, LANES), 1) < GROUPS
    stats = jnp.where(inside, jnp.where(pick == 0, mean, jnp.where(pick == 1, rstd, 0.0)), 0.0)
    spread = dot(stats, member, dims=((1,), (1,)), precision=lax.Precision.HIGHEST)
    normed = (tok_ref[...].astype(F32) - spread[0:1, :]) * spread[1:2, :]
    nrm[0:TOK, :] = (normed * gain_ref[...] + bias_ref[...]).astype(BF16)
    nrm_copy().start()

    z_wait(0)
    start(x_copies(*wave(0, x_s, x_r)))
    there = nrm.at[pl.ds(TOK, TOK)]
    remote(there, there, nrm_s, nrm_r, sib).wait_recv()

    low = lax.broadcasted_iota(jnp.int32, (TOK, LANES), 1) < LANES // 2

    def attend(g, which):
        query = qb[pl.ds(which * TOK, TOK), :]
        keys = kvb[g, 0, pl.ds(which * 2 * TOK, 4 * TOK), :]
        values = kvb[g, 1, pl.ds(which * 2 * TOK, 4 * TOK), :]
        values = jnp.concatenate([values, jnp.ones_like(values)], axis=1)
        results = []
        for head in range(2):
            own = jnp.where(low if head == 0 else ~low, query, jnp.zeros_like(query))
            scores = dot(own, keys, dims=((1,), (1,)))
            top = jnp.max(scores, axis=1, keepdims=True)
            weights = jnp.exp(scores - top).astype(BF16)
            both = dot(weights, values)
            results.append(both[:, :LANES] / both[:, LANES:])
        return jnp.where(low, results[0], results[1]).astype(BF16)

    def step(g, carry):
        @pl.when(g + 2 < WAVES)
        def _():
            start(z_copies(g + 2))
            start(kv_copies(g + 2))
            kv_own(g + 2).start()

        @pl.when(g == 1)
        def _():
            start(zo_copies())

        @pl.when(g + 1 < WAVES)
        def _():
            z_wait(g + 1)
            start(x_copies(*wave(g + 1, x_s, x_r)))

        @pl.when(g == 2)
        def _():
            zo_wait()
            start(x_copies(*owave(xo_s, xo_r)))

        x_wait(*wave(g, x_s, x_r))
        start(xx_copies(*wave(g, xx_s, xx_r)))

        @pl.when(g == 3)
        def _():
            x_wait(*owave(xo_s, xo_r))
            start(xx_copies(*owave(xxo_s, xxo_r)))

        xx_wait(*wave(g, xx_s, xx_r))

        for at in range(NX):
            heads = jnp.concatenate([w_buf[g, at, :, :, t].reshape(256, LANES) for t in range(3)], axis=1)
            part = dot(pick_a[...], heads)
            rest = w_buf[g, at, :, :, 3].reshape(256, LANES)
            for t in range(3):
                both = part[:, t * LANES : (t + 1) * LANES] + dot(pick_b[t], rest)
                w_nat[at * 320 : (at + 1) * 320, t * LANES : (t + 1) * LANES] = both.astype(BF16)
        result = dot(nrm[...], w_nat[...])
        qb[...] = (result[:, :LANES] * 0.125).astype(BF16)
        for t in range(2):
            new = result[:, (t + 1) * LANES : (t + 2) * LANES].astype(BF16)
            kvb[g, t, block(1)] = new[:TOK]
            kvb[g, t, block(4)] = new[TOK:]
        fkv_own(g).start()
        fkv_copy(g).start()
        kv_wait(g)

        ho_out[g] = attend(g, 1)
        ho_copy(g).start()
        ho[core * WAVES + g] = attend(g, 0)
        return carry

    lax.fori_loop(0, WAVES, step, 0)

    xx_wait(*owave(xxo_s, xxo_r))
    for at in range(NX):
        for g in range(WAVES):
            part = dot(pick_a[...], wo_buf[at, :, :, g].reshape(256, LANES))
            part = part + dot(pick_b[3], w_buf[g, at, :, :, 3].reshape(256, LANES))
            wo_nat[core, at * 320 : (at + 1) * 320, g * LANES : (g + 1) * LANES] = part.astype(BF16)
    won_copy().start()
    for g in range(WAVES):
        ho_wait(g)
    there = wo_nat.at[1 - core]
    remote(there, there, won_s, won_r, sib).wait_recv()
    lhs = jnp.concatenate([ho[i] for i in range(2 * WAVES)], axis=1)
    for i in range(2):
        att_ref[:, i * HALF : (i + 1) * HALF] = dot(lhs, wo_nat[i]).astype(BF16)

    for copy in mom_copies() + y_copies() + zo_copies() + [nrm_copy(), won_copy()]:
        copy.wait_send()
    for copy in x_copies(*owave(xo_s, xo_r)) + xx_copies(*owave(xxo_s, xxo_r)):
        copy.wait_send()

    def drain(g, carry):
        for copy in z_copies(g) + kv_copies(g) + [fkv_copy(g), ho_copy(g)]:
            copy.wait_send()
        for copy in x_copies(*wave(g, x_s, x_r)) + xx_copies(*wave(g, xx_s, xx_r)):
            copy.wait_send()
        fkv_wait(g)
        fkv_own(g).wait()
        return carry

    lax.fori_loop(0, WAVES, drain, 0)


def shards(tokens, stale_kv, stale_moments, norm_gain, norm_bias, w_query, w_key, w_value, w_out):
    vmem = pl.BlockSpec(memory_space=pltpu.VMEM)
    hbm = pl.BlockSpec(memory_space=pl.ANY)
    dma = pltpu.SemaphoreType.DMA
    z1 = NZ - 1
    attended, fresh_kv, sums, squares = pl.pallas_call(
        kernel,
        out_shape=(
            jax.ShapeDtypeStruct((TOK, CH), BF16),
            jax.ShapeDtypeStruct((2, TOK, CH), BF16),
            jax.ShapeDtypeStruct((1, GROUPS), F32),
            jax.ShapeDtypeStruct((1, GROUPS), F32),
        ),
        in_specs=[vmem, hbm] + [vmem] * 7,
        out_specs=(vmem, hbm, vmem, vmem),
        scratch_shapes=[
            pltpu.VMEM((WAVES, NX, NZ, NY, 4, 16, LANES), BF16),
            pltpu.VMEM((NX, NZ, NY, WAVES, 16, LANES), BF16),
            pltpu.VMEM((CH, 3 * LANES), BF16),
            pltpu.VMEM((2, CH, HALF), BF16),
            pltpu.VMEM((320, 256), BF16),
            pltpu.VMEM((4, 320, 256), BF16),
            pltpu.VMEM((16, HALF), F32),
            pltpu.VMEM((WAVES, 2, 6 * TOK, LANES), BF16),
            pltpu.VMEM((2 * TOK, CH), BF16),
            pltpu.VMEM((2 * TOK, LANES), BF16),
            pltpu.VMEM((2 * WAVES, TOK, LANES), BF16),
            pltpu.VMEM((WAVES, TOK, LANES), BF16),
            pltpu.VMEM((4, 8, LANES), F32),
            dma((2,)), dma((2,)),
            dma((WAVES, z1)), dma((WAVES, z1)),
            dma((WAVES, 2)), dma((WAVES, 2)),
            dma((WAVES, 2)), dma((WAVES, 2)),
            dma((z1,)), dma((z1,)),
            dma((2,)), dma((2,)),
            dma((2,)), dma((2,)),
            dma((WAVES, 3)), dma((WAVES, 3)), dma((WAVES,)),
            dma((3,)), dma((3,)),
            dma, dma,
            dma((WAVES,)), dma((WAVES,)), dma((WAVES,)),
            dma((WAVES,)), dma((WAVES,)),
            dma, dma,
        ],
        compiler_params=pltpu.CompilerParams(
            collective_id=0, has_side_effects=True, vmem_limit_bytes=60 << 20
        ),
        name="block",
    )(
        tokens.reshape(TOK, CH), stale_kv[0], stale_moments[0, 0],
        norm_gain[None], norm_bias[None], w_query, w_key, w_value, w_out,
    )
    return (
        attended.reshape(tokens.shape),
        fresh_kv[None],
        sums[None],
        squares[None],
    )


def solution(mesh):
    in_specs = (
        P("rows", None, "strips", None),
        P("rows", None, "strips", None),
        P("rows", "strips", None, None),
        P(),
        P(),
        P("rows", None),
        P("rows", None),
        P("rows", None),
        P("rows", None),
    )
    out_specs = (
        P("rows", None, "strips", None),
        P("rows", None, "strips", None),
        P("rows", "strips", None),
        P("rows", "strips", None),
    )
    return jax.shard_map(shards, mesh=mesh, in_specs=in_specs, out_specs=out_specs, check_vma=False)
```

```python
import jax
import jax.numpy as jnp
from jax import lax
from jax.experimental import pallas as pl
from jax.experimental.pallas import tpu as pltpu
from jax.sharding import PartitionSpec as P

MESH = pl.DeviceIdType.MESH
F32 = jnp.float32
BF16 = jnp.bfloat16

TOK = 384
CH = 1280
HALF = 640
LANES = 128
WAVES = 5
NX, NZ, NY = 4, 8, 2
SHARD = 20
GROUPS = 32
PER_GROUP = 40


def dot(a, b, dims=((1,), (0,)), precision=None):
    return lax.dot_general(a, b, (dims, ((), ())), precision=precision, preferred_element_type=F32)


def kernel(
    tok_ref, kv_ref, mom_ref, gain_ref, bias_ref, wq_ref, wk_ref, wv_ref, wo_ref,
    att_ref, fkv_ref, fs_ref, fq_ref,
    w_buf, wo_buf, w_nat, wo_nat, pick_a, pick_b, tail, kvb, nrm, qb, ho, ho_out, moms,
    y_s, y_r, z_s, z_r, x_s, x_r, xx_s, xx_r, ox_s, ox_r, oz_s, oz_r,
    kv_s, kv_r, kv_l, mom_s, mom_r, nrm_s, nrm_r, fkv_s, fkv_r, fkv_l, ho_s, ho_r, won_s, won_r,
):
    row = lax.axis_index("rows")
    strip = lax.axis_index("strips")
    ylo = row % 2
    z = (row // 2) % NZ
    x = row // (2 * NZ)
    core = strip % 2
    yhi = strip // 2

    sib = (row, yhi * 2 + 1 - core)
    far = (row, (1 - yhi) * 2 + core)
    far_other = (row, (1 - yhi) * 2 + 1 - core)
    y_peer = (x * 16 + z * 2 + 1 - ylo, strip)
    z_peers = [(x * 16 + ((z + d) % NZ) * 2 + ylo, strip) for d in range(1, NZ)]
    xl = (x + NX - 1) % NX
    xr = (x + 1) % NX
    x_far = (x + 2) % NX
    x_left = (xl * 16 + z * 2 + ylo, strip)
    x_right = (xr * 16 + z * 2 + ylo, strip)
    x_across = (x_far * 16 + z * 2 + ylo, strip)

    barrier = pltpu.get_barrier_semaphore()
    everyone = [sib, far, far_other, y_peer, x_left, x_right, x_across] + z_peers
    for peer in everyone:
        pl.semaphore_signal(barrier, inc=1, device_id=peer, device_id_type=MESH)

    def remote(src, dst, send, recv, to):
        return pltpu.make_async_remote_copy(
            src_ref=src, dst_ref=dst, send_sem=send, recv_sem=recv, device_id=to, device_id_type=MESH
        )

    mine = pl.ds(pl.multiple_of(core * HALF, LANES), HALF)
    for t, ref in enumerate((wq_ref, wk_ref, wv_ref, wo_ref)):
        rows = ref[:, mine]
        for g in range(WAVES):
            piece = rows[:16, g * LANES : (g + 1) * LANES]
            if t < 3:
                w_buf[g, x, z, ylo, t] = piece
            else:
                wo_buf[z, x, ylo, g] = piece
        tail[4 * t : 4 * t + 4, :] = rows.astype(F32)[16:SHARD, :]
    rest = tail[...].astype(BF16)
    for g in range(WAVES):
        w_buf[g, x, z, ylo, 3] = rest[:, g * LANES : (g + 1) * LANES]
    moms[0] = jnp.zeros((8, LANES), F32)
    moms[0, 0:2, 0:GROUPS] = mom_ref[...]

    pl.semaphore_wait(barrier, len(everyone))

    def y_copies():
        here = w_buf.at[:, x, z, ylo]
        ohere = wo_buf.at[z, x, ylo]
        return [
            remote(here, here, y_s.at[0], y_r.at[0], y_peer),
            remote(ohere, ohere, y_s.at[1], y_r.at[1], y_peer),
        ]

    def y_wait():
        there = w_buf.at[:, x, z, 1 - ylo]
        othere = wo_buf.at[z, x, 1 - ylo]
        remote(there, there, y_s.at[0], y_r.at[0], y_peer).wait_recv()
        remote(othere, othere, y_s.at[1], y_r.at[1], y_peer).wait_recv()

    def z_copies(g):
        return [
            remote(w_buf.at[g, x, z], w_buf.at[g, x, z], z_s.at[g, d], z_r.at[g, d], z_peers[d])
            for d in range(NZ - 1)
        ]

    def z_wait(g):
        for d in range(NZ - 1):
            there = w_buf.at[g, x, (z + NZ - 1 - d) % NZ]
            remote(there, there, z_s.at[g, d], z_r.at[g, d], z_peers[d]).wait_recv()

    def ox_copies():
        here = wo_buf.at[z, x]
        return [
            remote(here, here, ox_s.at[i], ox_r.at[i], to) for i, to in enumerate((x_right, x_across, x_left))
        ]

    def ox_wait():
        for i, at in enumerate((xl, x_far, xr)):
            there = wo_buf.at[z, at]
            remote(there, there, ox_s.at[i], ox_r.at[i], x_right).wait_recv()

    def z_at(d):
        return (z + NZ + d) % NZ

    def z_peer(d):
        return z_peers[(d - 1) % NZ]

    def oz_copies():
        here = wo_buf.at[z]
        return [remote(here, here, oz_s.at[i], oz_r.at[i], z_peer(d)) for i, d in enumerate((1, -1, 2, -2))]

    def ozz_copies():
        left, right = wo_buf.at[z_at(-2)], wo_buf.at[z_at(2)]
        left_half, right_half = wo_buf.at[z_at(-2), pl.ds(0, 2)], wo_buf.at[z_at(2), pl.ds(2, 2)]
        return [
            remote(ref, ref, oz_s.at[i + 4], oz_r.at[i + 4], z_peer(d))
            for i, (ref, d) in enumerate(((left, 1), (right, -1), (left_half, 2), (right_half, -2)))
        ]

    def oz_wait(which):
        for i in which:
            there = wo_buf.at[z_at((-1, 1, -2, 2, -3, 3, 4, 4)[i])]
            if i >= 6:
                there = wo_buf.at[z_at(4), pl.ds(2 * (i - 6), 2)]
            remote(there, there, oz_s.at[i], oz_r.at[i], x_right).wait_recv()

    def x_copies(g):
        here = w_buf.at[g, x]
        return [
            remote(here, here, x_s.at[g, 0], x_r.at[g, 0], x_right),
            remote(here, here, x_s.at[g, 1], x_r.at[g, 1], x_left),
        ]

    def x_wait(g):
        for i, at in ((0, xl), (1, xr)):
            there = w_buf.at[g, at]
            remote(there, there, x_s.at[g, i], x_r.at[g, i], x_right).wait_recv()

    def xx_copies(g):
        first, second = w_buf.at[g, xl, pl.ds(0, NZ // 2)], w_buf.at[g, xr, pl.ds(NZ // 2, NZ // 2)]
        return [
            remote(first, first, xx_s.at[g, 0], xx_r.at[g, 0], x_right),
            remote(second, second, xx_s.at[g, 1], xx_r.at[g, 1], x_left),
        ]

    def xx_wait(g):
        for i in (0, 1):
            there = w_buf.at[g, x_far, pl.ds(i * (NZ // 2), NZ // 2)]
            remote(there, there, xx_s.at[g, i], xx_r.at[g, i], x_right).wait_recv()

    def lanes(which, g):
        return pl.ds(pl.multiple_of(which * HALF + g * LANES, LANES), LANES)

    def block(i):
        return pl.ds(i * TOK, TOK)

    def kv_copies(g):
        mine_g, other_g = kv_ref.at[:, :, lanes(core, g)], kv_ref.at[:, :, lanes(1 - core, g)]
        return [
            remote(other_g, kvb.at[g, :, block(0)], kv_s.at[g, 0], kv_r.at[g, 0], sib),
            remote(mine_g, kvb.at[g, :, block(2)], kv_s.at[g, 1], kv_r.at[g, 1], far),
            remote(other_g, kvb.at[g, :, block(3)], kv_s.at[g, 2], kv_r.at[g, 2], far_other),
        ]

    def kv_own(g):
        return pltpu.make_async_copy(kv_ref.at[:, :, lanes(core, g)], kvb.at[g, :, block(5)], kv_l.at[g])

    def kv_wait(g):
        for i, b in enumerate((0, 2, 3)):
            there = kvb.at[g, :, block(b)]
            remote(there, there, kv_s.at[g, i], kv_r.at[g, i], sib).wait_recv()
        kv_own(g).wait()

    def mom_copies():
        return [
            remote(moms.at[0], moms.at[i + 1], mom_s.at[i], mom_r.at[i], to)
            for i, to in enumerate((sib, far, far_other))
        ]

    def nrm_copy():
        return remote(nrm.at[pl.ds(0, TOK)], nrm.at[pl.ds(TOK, TOK)], nrm_s, nrm_r, sib)

    def fkv_copy(g):
        return remote(kvb.at[g, :, block(4)], fkv_ref.at[:, :, lanes(core, g)], fkv_s.at[g], fkv_r.at[g], sib)

    def fkv_own(g):
        return pltpu.make_async_copy(kvb.at[g, :, block(1)], fkv_ref.at[:, :, lanes(core, g)], fkv_l.at[g])

    def fkv_wait(g):
        there = fkv_ref.at[:, :, lanes(1 - core, g)]
        remote(there, there, fkv_s.at[g], fkv_r.at[g], sib).wait_recv()

    def ho_copy(g):
        return remote(ho_out.at[g], ho.at[core * WAVES + g], ho_s.at[g], ho_r.at[g], sib)

    def ho_wait(g):
        there = ho.at[(1 - core) * WAVES + g]
        remote(there, there, ho_s.at[g], ho_r.at[g], sib).wait_recv()

    def won_copy():
        return remote(wo_nat.at[core], wo_nat.at[core], won_s, won_r, sib)

    def start(copies):
        for copy in copies:
            copy.start()

    def kv_start(g):
        start(kv_copies(g))
        kv_own(g).start()

    start(y_copies())
    start(mom_copies())
    kv_start(0)

    channel = lax.broadcasted_iota(jnp.int32, (CH, LANES), 0)
    group = lax.broadcasted_iota(jnp.int32, (CH, LANES), 1)
    member = jnp.where((channel >= group * PER_GROUP) & (channel < (group + 1) * PER_GROUP), 1.0, 0.0)
    toks = tok_ref[...].astype(F32)
    sums = jnp.sum(toks, axis=0, keepdims=True)
    squares = jnp.sum(toks * toks, axis=0, keepdims=True)
    pick = lax.broadcasted_iota(jnp.int32, (8, CH), 0)
    stacked = jnp.where(pick == 0, sums, jnp.where(pick == 1, squares, 0.0))
    fresh = dot(stacked, member, precision=lax.Precision.HIGHEST)
    fs_ref[...] = fresh[0:1, 0:GROUPS]
    fq_ref[...] = fresh[1:2, 0:GROUPS]

    y_wait()
    start(z_copies(0))
    start(ox_copies())
    kv_start(1)
    kv_start(2)
    start(z_copies(1))

    k_at = lax.broadcasted_iota(jnp.int32, (320, 256), 0)
    j_at = lax.broadcasted_iota(jnp.int32, (320, 256), 1)
    base = (j_at >> 4) * SHARD
    pick_a[...] = jnp.where(k_at == base + (j_at & 15), 1.0, 0.0).astype(BF16)
    for t in range(4):
        hit = (k_at == base + 16 + (j_at & 3)) & (((j_at >> 2) & 3) == t)
        pick_b[t] = jnp.where(hit, 1.0, 0.0).astype(BF16)

    for i in range(3):
        there = moms.at[i + 1]
        remote(there, there, mom_s.at[i], mom_r.at[i], sib).wait_recv()
    mixed = (moms[1] + moms[2] + moms[3]) + fresh
    count = float(TOK * 4 * PER_GROUP)
    mean = mixed[0:1, :] / count
    var = mixed[1:2, :] / count - mean * mean
    rstd = lax.rsqrt(var + 1e-05)
    pick = lax.broadcasted_iota(jnp.int32, (8, LANES), 0)
    inside = lax.broadcasted_iota(jnp.int32, (8, LANES), 1) < GROUPS
    stats = jnp.where(inside, jnp.where(pick == 0, mean, jnp.where(pick == 1, rstd, 0.0)), 0.0)
    spread = dot(stats, member, dims=((1,), (1,)), precision=lax.Precision.HIGHEST)
    normed = (tok_ref[...].astype(F32) - spread[0:1, :]) * spread[1:2, :]
    nrm[0:TOK, :] = (normed * gain_ref[...][None] + bias_ref[...][None]).astype(BF16)
    nrm_copy().start()

    z_wait(0)
    start(x_copies(0))
    start(z_copies(2))
    z_wait(1)
    start(x_copies(1))
    x_wait(0)
    start(xx_copies(0))
    there = nrm.at[pl.ds(TOK, TOK)]
    remote(there, there, nrm_s, nrm_r, sib).wait_recv()

    low = lax.broadcasted_iota(jnp.int32, (TOK, LANES), 1) < LANES // 2

    def attend(g, which):
        query = qb[pl.ds(which * TOK, TOK), :]
        keys = kvb[g, 0, pl.ds(which * 2 * TOK, 4 * TOK), :]
        values = kvb[g, 1, pl.ds(which * 2 * TOK, 4 * TOK), :]
        values = jnp.concatenate([values, jnp.ones_like(values)], axis=1)
        results = []
        for head in range(2):
            own = jnp.where(low if head == 0 else ~low, query, jnp.zeros_like(query))
            scores = dot(own, keys, dims=((1,), (1,)))
            top = jnp.max(scores, axis=1, keepdims=True)
            weights = jnp.exp(scores - top).astype(BF16)
            both = dot(weights, values)
            results.append(both[:, :LANES] / both[:, LANES:])
        return jnp.where(low, results[0], results[1]).astype(BF16)

    def step(g, carry):
        @pl.when(g + 3 < WAVES)
        def _():
            start(z_copies(g + 3))
            kv_start(g + 3)

        @pl.when(g == 1)
        def _():
            ox_wait()
            start(oz_copies())

        @pl.when(g + 2 < WAVES)
        def _():
            z_wait(g + 2)
            start(x_copies(g + 2))

        @pl.when(g + 1 < WAVES)
        def _():
            x_wait(g + 1)
            start(xx_copies(g + 1))

        @pl.when(g == 3)
        def _():
            oz_wait((2, 3))
            start(ozz_copies())

        xx_wait(g)

        for at in range(NX):
            heads = jnp.concatenate([w_buf[g, at, :, :, t].reshape(256, LANES) for t in range(3)], axis=1)
            part = dot(pick_a[...], heads)
            rest = w_buf[g, at, :, :, 3].reshape(256, LANES)
            for t in range(3):
                both = part[:, t * LANES : (t + 1) * LANES] + dot(pick_b[t], rest)
                w_nat[at * 320 : (at + 1) * 320, t * LANES : (t + 1) * LANES] = both.astype(BF16)
        result = dot(nrm[...], w_nat[...])
        qb[...] = (result[:, :LANES] * 0.125).astype(BF16)
        for t in range(2):
            new = result[:, (t + 1) * LANES : (t + 2) * LANES].astype(BF16)
            kvb[g, t, block(1)] = new[:TOK]
            kvb[g, t, block(4)] = new[TOK:]
        fkv_own(g).start()
        fkv_copy(g).start()
        kv_wait(g)

        @pl.when(g == WAVES - 1)
        def _():
            oz_wait((0, 1, 4, 5, 6, 7))
            both_picks = jnp.concatenate([pick_a[...], pick_b[3]], axis=1)
            for at in range(NX):
                heads = [wo_buf[:, at, :, i].reshape(256, LANES) for i in range(WAVES)]
                rest = [w_buf[i, at, :, :, 3].reshape(256, LANES) for i in range(WAVES)]
                stack = jnp.concatenate([jnp.concatenate(heads, axis=1), jnp.concatenate(rest, axis=1)], axis=0)
                wo_nat[core, at * 320 : (at + 1) * 320, :] = dot(both_picks, stack).astype(BF16)
            won_copy().start()

        ho_out[g] = attend(g, 1)
        ho_copy(g).start()
        ho[core * WAVES + g] = attend(g, 0)
        return carry

    lax.fori_loop(0, WAVES, step, 0)

    for g in range(WAVES):
        ho_wait(g)
    there = wo_nat.at[1 - core]
    remote(there, there, won_s, won_r, sib).wait_recv()
    lhs = jnp.concatenate([ho[i] for i in range(2 * WAVES)], axis=1)
    for i in range(2):
        att_ref[:, i * HALF : (i + 1) * HALF] = dot(lhs, wo_nat[i]).astype(BF16)

    for copy in mom_copies() + y_copies() + ox_copies() + oz_copies() + ozz_copies() + [nrm_copy(), won_copy()]:
        copy.wait_send()

    def drain(g, carry):
        for copy in z_copies(g) + x_copies(g) + xx_copies(g) + kv_copies(g) + [fkv_copy(g), ho_copy(g)]:
            copy.wait_send()
        fkv_wait(g)
        fkv_own(g).wait()
        return carry

    lax.fori_loop(0, WAVES, drain, 0)


def shards(tokens, stale_kv, stale_moments, norm_gain, norm_bias, w_query, w_key, w_value, w_out):
    vmem = pl.BlockSpec(memory_space=pltpu.VMEM)
    hbm = pl.BlockSpec(memory_space=pl.ANY)
    dma = pltpu.SemaphoreType.DMA
    z1 = NZ - 1
    attended, fresh_kv, sums, squares = pl.pallas_call(
        kernel,
        out_shape=(
            jax.ShapeDtypeStruct((TOK, CH), BF16),
            jax.ShapeDtypeStruct((2, TOK, CH), BF16),
            jax.ShapeDtypeStruct((1, GROUPS), F32),
            jax.ShapeDtypeStruct((1, GROUPS), F32),
        ),
        in_specs=[vmem, hbm] + [vmem] * 7,
        out_specs=(vmem, hbm, vmem, vmem),
        scratch_shapes=[
            pltpu.VMEM((WAVES, NX, NZ, NY, 4, 16, LANES), BF16),
            pltpu.VMEM((NZ, NX, NY, WAVES, 16, LANES), BF16),
            pltpu.VMEM((CH, 3 * LANES), BF16),
            pltpu.VMEM((2, CH, HALF), BF16),
            pltpu.VMEM((320, 256), BF16),
            pltpu.VMEM((4, 320, 256), BF16),
            pltpu.VMEM((16, HALF), F32),
            pltpu.VMEM((WAVES, 2, 6 * TOK, LANES), BF16),
            pltpu.VMEM((2 * TOK, CH), BF16),
            pltpu.VMEM((2 * TOK, LANES), BF16),
            pltpu.VMEM((2 * WAVES, TOK, LANES), BF16),
            pltpu.VMEM((WAVES, TOK, LANES), BF16),
            pltpu.VMEM((4, 8, LANES), F32),
            dma((2,)), dma((2,)),
            dma((WAVES, z1)), dma((WAVES, z1)),
            dma((WAVES, 2)), dma((WAVES, 2)),
            dma((WAVES, 2)), dma((WAVES, 2)),
            dma((3,)), dma((3,)),
            dma((8,)), dma((8,)),
            dma((WAVES, 3)), dma((WAVES, 3)), dma((WAVES,)),
            dma((3,)), dma((3,)),
            dma, dma,
            dma((WAVES,)), dma((WAVES,)), dma((WAVES,)),
            dma((WAVES,)), dma((WAVES,)),
            dma, dma,
        ],
        compiler_params=pltpu.CompilerParams(
            collective_id=0, has_side_effects=True, vmem_limit_bytes=60 << 20
        ),
        name="block",
    )(
        tokens.reshape(TOK, CH), stale_kv[0], stale_moments[0, 0],
        norm_gain, norm_bias, w_query, w_key, w_value, w_out,
    )
    return (
        attended.reshape(tokens.shape),
        fresh_kv[None],
        sums[None],
        squares[None],
    )


def solution(mesh):
    in_specs = (
        P("rows", None, "strips", None),
        P("rows", None, "strips", None),
        P("rows", "strips", None, None),
        P(),
        P(),
        P("rows", None),
        P("rows", None),
        P("rows", None),
        P("rows", None),
    )
    out_specs = (
        P("rows", None, "strips", None),
        P("rows", None, "strips", None),
        P("rows", "strips", None),
        P("rows", "strips", None),
    )
    return jax.shard_map(shards, mesh=mesh, in_specs=in_specs, out_specs=out_specs, check_vma=False)
```

```python
import jax
import jax.numpy as jnp
from jax import lax
from jax.experimental import pallas as pl
from jax.experimental.pallas import tpu as pltpu
from jax.sharding import PartitionSpec as P

MESH = pl.DeviceIdType.MESH
F32 = jnp.float32
BF16 = jnp.bfloat16

TOK = 384
CH = 1280
HALF = 640
LANES = 128
WAVES = 5
RING = 1
DIRECT = WAVES - 1
NX, NZ, NY = 4, 8, 2
SHARD = 20
GROUPS = 32
PER_GROUP = 40


def dot(a, b, dims=((1,), (0,)), precision=None):
    return lax.dot_general(a, b, (dims, ((), ())), precision=precision, preferred_element_type=F32)


def kernel(
    tok_ref, kv_ref, mom_ref, gain_ref, bias_ref, wq_ref, wk_ref, wv_ref, wo_ref,
    att_ref, fkv_ref, fs_ref, fq_ref,
    w_buf, b_buf, o_buf, w_nat, wo_nat, picks, part_pick, order, tail, kvb, nrm, qb, ho, ho_out, moms,
    y_s, y_r, z_s, z_r, x_s, x_r, xx_s, xx_r, bx_s, bx_r, bz_s, bz_r, ox_s, ox_r, oz_s, oz_r,
    kv_s, kv_r, kv_l, mom_s, mom_r, nrm_s, nrm_r, fkv_s, fkv_r, fkv_l, ho_s, ho_r, won_s, won_r,
):
    row = lax.axis_index("rows")
    strip = lax.axis_index("strips")
    ylo = row % 2
    z = (row // 2) % NZ
    x = row // (2 * NZ)
    core = strip % 2
    yhi = strip // 2

    sib = (row, yhi * 2 + 1 - core)
    far = (row, (1 - yhi) * 2 + core)
    far_other = (row, (1 - yhi) * 2 + 1 - core)
    y_peer = (x * 16 + z * 2 + 1 - ylo, strip)

    def z_at(d):
        return (z + NZ + d) % NZ

    def z_peer(d):
        return (x * 16 + z_at(d) * 2 + ylo, strip)

    xl = (x + NX - 1) % NX
    xr = (x + 1) % NX
    x_far = (x + 2) % NX
    x_left = (xl * 16 + z * 2 + ylo, strip)
    x_right = (xr * 16 + z * 2 + ylo, strip)
    x_across = (x_far * 16 + z * 2 + ylo, strip)

    barrier = pltpu.get_barrier_semaphore()
    everyone = [sib, far, far_other, y_peer, x_left, x_right, x_across] + [z_peer(d) for d in (1, -1, 2, -2)]
    for peer in everyone:
        pl.semaphore_signal(barrier, inc=1, device_id=peer, device_id_type=MESH)

    def remote(src, dst, send, recv, to):
        return pltpu.make_async_remote_copy(
            src_ref=src, dst_ref=dst, send_sem=send, recv_sem=recv, device_id=to, device_id_type=MESH
        )

    mine = pl.ds(pl.multiple_of(core * HALF, LANES), HALF)
    for t, ref in enumerate((wq_ref, wk_ref, wv_ref, wo_ref)):
        rows = ref[:, mine]
        for g in range(WAVES):
            piece = rows[:16, g * LANES : (g + 1) * LANES]
            if t == 3:
                o_buf[z, x, ylo, g] = piece
            elif g == RING:
                b_buf[z, x, ylo, t] = piece
            else:
                w_buf[g - (g > RING), x, z, ylo, t] = piece
        tail[4 * t : 4 * t + 4, :] = rows.astype(F32)[16:SHARD, :]
    rest = tail[...].astype(BF16)
    for g in range(WAVES):
        piece = rest[:, g * LANES : (g + 1) * LANES]
        if g == RING:
            b_buf[z, x, ylo, 3] = piece
        else:
            w_buf[g - (g > RING), x, z, ylo, 3] = piece
    moms[0] = jnp.zeros((8, LANES), F32)
    moms[0, 0:2, 0:GROUPS] = mom_ref[...]

    pl.semaphore_wait(barrier, len(everyone))

    def y_refs(side):
        return (
            w_buf.at[0, x, z, side],
            b_buf.at[z, x, side],
            w_buf.at[pl.ds(1, DIRECT - 1), x, z, side],
            o_buf.at[z, x, side],
        )

    def y_copies():
        return [remote(ref, ref, y_s.at[i], y_r.at[i], y_peer) for i, ref in enumerate(y_refs(ylo))]

    def y_wait(i):
        there = y_refs(1 - ylo)[i]
        remote(there, there, y_s.at[i], y_r.at[i], y_peer).wait_recv()

    def z_copies(g):
        here = w_buf.at[g, x, z]
        return [
            remote(here, here, z_s.at[g, i], z_r.at[g, i], z_peer(d)) for i, d in enumerate((1, -1, 2, -2))
        ]

    def zz_copies(g):
        left, right = w_buf.at[g, x, z_at(-2)], w_buf.at[g, x, z_at(2)]
        left_half, right_half = w_buf.at[g, x, z_at(-2), 0], w_buf.at[g, x, z_at(2), 1]
        return [
            remote(ref, ref, z_s.at[g, i + 4], z_r.at[g, i + 4], z_peer(d))
            for i, (ref, d) in enumerate(((left, 1), (right, -1), (left_half, 2), (right_half, -2)))
        ]

    def z_wait(g, which):
        for i in which:
            there = w_buf.at[g, x, z_at((-1, 1, -2, 2, -3, 3)[i])] if i < 6 else w_buf.at[g, x, z_at(4), i - 6]
            remote(there, there, z_s.at[g, i], z_r.at[g, i], x_right).wait_recv()

    class Ring:
        def __init__(self, buf, x_send, x_recv, send, recv):
            self.buf, self.x_send, self.x_recv, self.send, self.recv = buf, x_send, x_recv, send, recv

        def x_copies(self):
            here = self.buf.at[z, x]
            return [
                remote(here, here, self.x_send.at[i], self.x_recv.at[i], to)
                for i, to in enumerate((x_right, x_across, x_left))
            ]

        def x_wait(self):
            for i, at in enumerate((xl, x_far, xr)):
                there = self.buf.at[z, at]
                remote(there, there, self.x_send.at[i], self.x_recv.at[i], x_right).wait_recv()

        def refs(self, step):
            if step < 3:
                return self.buf.at[z_at(-1 - step)], self.buf.at[z_at(1 + step)]
            return self.buf.at[z_at(4), pl.ds(0, 2)], self.buf.at[z_at(4), pl.ds(2, 2)]

        def copies(self, step):
            if step == 0:
                refs = self.buf.at[z], self.buf.at[z]
            elif step < 3:
                refs = self.refs(step - 1)
            else:
                refs = self.buf.at[z_at(-3), pl.ds(0, 2)], self.buf.at[z_at(3), pl.ds(2, 2)]
            return [
                remote(ref, ref, self.send.at[2 * step + i], self.recv.at[2 * step + i], z_peer(d))
                for i, (ref, d) in enumerate(zip(refs, (1, -1)))
            ]

        def wait(self, step):
            for i, there in enumerate(self.refs(step)):
                remote(there, there, self.send.at[2 * step + i], self.recv.at[2 * step + i], x_right).wait_recv()

        def go(self, step):
            if step == 0:
                self.x_wait()
            else:
                self.wait(step - 1)
            start(self.copies(step))

        def drain(self):
            for copy in self.x_copies() + [c for step in range(4) for c in self.copies(step)]:
                copy.wait_send()

    b_ring = Ring(b_buf, bx_s, bx_r, bz_s, bz_r)
    o_ring = Ring(o_buf, ox_s, ox_r, oz_s, oz_r)

    def x_copies(g):
        here = w_buf.at[g, x]
        return [
            remote(here, here, x_s.at[g, 0], x_r.at[g, 0], x_right),
            remote(here, here, x_s.at[g, 1], x_r.at[g, 1], x_left),
        ]

    def x_wait(g):
        for i, at in ((0, xl), (1, xr)):
            there = w_buf.at[g, at]
            remote(there, there, x_s.at[g, i], x_r.at[g, i], x_right).wait_recv()

    def xx_copies(g):
        first, second = w_buf.at[g, xl, pl.ds(0, NZ // 2)], w_buf.at[g, xr, pl.ds(NZ // 2, NZ // 2)]
        return [
            remote(first, first, xx_s.at[g, 0], xx_r.at[g, 0], x_right),
            remote(second, second, xx_s.at[g, 1], xx_r.at[g, 1], x_left),
        ]

    def xx_wait(g):
        for i in (0, 1):
            there = w_buf.at[g, x_far, pl.ds(i * (NZ // 2), NZ // 2)]
            remote(there, there, xx_s.at[g, i], xx_r.at[g, i], x_right).wait_recv()

    def lanes(which, g):
        return pl.ds(pl.multiple_of(which * HALF + g * LANES, LANES), LANES)

    def block(i):
        return pl.ds(i * TOK, TOK)

    def kv_copies(g):
        mine_g, other_g = kv_ref.at[:, :, lanes(core, g)], kv_ref.at[:, :, lanes(1 - core, g)]
        return [
            remote(other_g, kvb.at[g, :, block(0)], kv_s.at[g, 0], kv_r.at[g, 0], sib),
            remote(mine_g, kvb.at[g, :, block(2)], kv_s.at[g, 1], kv_r.at[g, 1], far),
            remote(other_g, kvb.at[g, :, block(3)], kv_s.at[g, 2], kv_r.at[g, 2], far_other),
        ]

    def kv_own(g):
        return pltpu.make_async_copy(kv_ref.at[:, :, lanes(core, g)], kvb.at[g, :, block(5)], kv_l.at[g])

    def kv_wait(g):
        for i, b in enumerate((0, 2, 3)):
            there = kvb.at[g, :, block(b)]
            remote(there, there, kv_s.at[g, i], kv_r.at[g, i], sib).wait_recv()
        kv_own(g).wait()

    def mom_copies():
        return [
            remote(moms.at[0], moms.at[i + 1], mom_s.at[i], mom_r.at[i], to)
            for i, to in enumerate((sib, far, far_other))
        ]

    def nrm_copy():
        return remote(nrm.at[pl.ds(0, TOK)], nrm.at[pl.ds(TOK, TOK)], nrm_s, nrm_r, sib)

    def fkv_copy(g):
        return remote(kvb.at[g, :, block(4)], fkv_ref.at[:, :, lanes(core, g)], fkv_s.at[g], fkv_r.at[g], sib)

    def fkv_own(g):
        return pltpu.make_async_copy(kvb.at[g, :, block(1)], fkv_ref.at[:, :, lanes(core, g)], fkv_l.at[g])

    def fkv_wait(g):
        there = fkv_ref.at[:, :, lanes(1 - core, g)]
        remote(there, there, fkv_s.at[g], fkv_r.at[g], sib).wait_recv()

    def ho_copy(g):
        return remote(ho_out.at[g], ho.at[core * WAVES + g], ho_s.at[g], ho_r.at[g], sib)

    def ho_wait(g):
        there = ho.at[(1 - core) * WAVES + g]
        remote(there, there, ho_s.at[g], ho_r.at[g], sib).wait_recv()

    def won_copy():
        return remote(wo_nat.at[core], wo_nat.at[core], won_s, won_r, sib)

    def start(copies):
        for copy in copies:
            copy.start()

    def kv_start(g):
        start(kv_copies(g))
        kv_own(g).start()

    def za(g):
        start(z_copies(g))

    def zb(g):
        z_wait(g, (2, 3))
        start(zz_copies(g))

    def xa(g):
        z_wait(g, (0, 1, 4, 5, 6, 7))
        start(x_copies(g))

    def xb(g):
        x_wait(g)
        start(xx_copies(g))

    start(y_copies())
    start(mom_copies())
    kv_start(0)

    channel = lax.broadcasted_iota(jnp.int32, (CH, LANES), 0)
    group = lax.broadcasted_iota(jnp.int32, (CH, LANES), 1)
    member = jnp.where((channel >= group * PER_GROUP) & (channel < (group + 1) * PER_GROUP), 1.0, 0.0)
    toks = tok_ref[...].astype(F32)
    sums = jnp.sum(toks, axis=0, keepdims=True)
    squares = jnp.sum(toks * toks, axis=0, keepdims=True)
    pick = lax.broadcasted_iota(jnp.int32, (8, CH), 0)
    stacked = jnp.where(pick == 0, sums, jnp.where(pick == 1, squares, 0.0))
    fresh = dot(stacked, member, precision=lax.Precision.HIGHEST)
    fs_ref[...] = fresh[0:1, 0:GROUPS]
    fq_ref[...] = fresh[1:2, 0:GROUPS]

    y_wait(0)
    za(0)
    y_wait(1)
    start(b_ring.x_copies())
    kv_start(1)
    kv_start(2)

    k_at = lax.broadcasted_iota(jnp.int32, (HALF, HALF), 0)
    j_at = lax.broadcasted_iota(jnp.int32, (HALF, HALF), 1)
    first = (j_at >> 8) * 320 + ((j_at & 255) >> 4) * SHARD + (j_at & 15)
    j_at = j_at - 512
    last = (j_at >> 6) * 320 + ((j_at & 63) >> 2) * SHARD + 16 + (j_at & 3)
    order[...] = jnp.where(k_at == jnp.where(j_at < 0, first, last), 1.0, 0.0).astype(BF16)
    r_at = lax.broadcasted_iota(jnp.int32, (192, 256), 0)
    j_at = lax.broadcasted_iota(jnp.int32, (192, 256), 1)
    hit = j_at == ((r_at & 63) >> 2) * 16 + (r_at >> 6) * 4 + (r_at & 3)
    part_pick[...] = jnp.where(hit, 1.0, 0.0).astype(BF16)

    zb(0)
    b_ring.go(0)

    for i in range(3):
        there = moms.at[i + 1]
        remote(there, there, mom_s.at[i], mom_r.at[i], sib).wait_recv()
    mixed = (moms[1] + moms[2] + moms[3]) + fresh
    count = float(TOK * 4 * PER_GROUP)
    mean = mixed[0:1, :] / count
    var = mixed[1:2, :] / count - mean * mean
    rstd = lax.rsqrt(var + 1e-05)
    pick = lax.broadcasted_iota(jnp.int32, (8, LANES), 0)
    inside = lax.broadcasted_iota(jnp.int32, (8, LANES), 1) < GROUPS
    stats = jnp.where(inside, jnp.where(pick == 0, mean, jnp.where(pick == 1, rstd, 0.0)), 0.0)
    spread = dot(stats, member, dims=((1,), (1,)), precision=lax.Precision.HIGHEST)
    normed = (tok_ref[...].astype(F32) - spread[0:1, :]) * spread[1:2, :]
    normed = (normed * gain_ref[...][None] + bias_ref[...][None]).astype(BF16)
    for i in range(2):
        moved = dot(normed[:, i * HALF : (i + 1) * HALF], order[...]).astype(BF16)
        nrm[0:TOK, i * 512 : (i + 1) * 512] = moved[:, :512]
        nrm[0:TOK, 1024 + i * LANES : 1024 + (i + 1) * LANES] = moved[:, 512:]
    nrm_copy().start()

    xa(0)
    y_wait(2)
    y_wait(3)
    za(1)
    b_ring.go(1)
    k_at = lax.broadcasted_iota(jnp.int32, (320, 256), 0)
    j_at = lax.broadcasted_iota(jnp.int32, (320, 256), 1)
    base = (j_at >> 4) * SHARD
    picks[:, :256] = jnp.where(k_at == base + (j_at & 15), 1.0, 0.0).astype(BF16)
    hit = (k_at == base + 16 + (j_at & 3)) & (((j_at >> 2) & 3) == 3)
    picks[:, 256:] = jnp.where(hit, 1.0, 0.0).astype(BF16)
    zb(1)
    za(2)
    b_ring.go(2)
    xb(0)
    xa(1)
    zb(2)
    b_ring.go(3)
    za(3)
    start(o_ring.x_copies())
    there = nrm.at[pl.ds(TOK, TOK)]
    remote(there, there, nrm_s, nrm_r, sib).wait_recv()

    low = lax.broadcasted_iota(jnp.int32, (TOK, LANES), 1) < LANES // 2

    def attend(g, which):
        query = qb[pl.ds(which * TOK, TOK), :]
        keys = kvb[g, 0, pl.ds(which * 2 * TOK, 4 * TOK), :]
        values = kvb[g, 1, pl.ds(which * 2 * TOK, 4 * TOK), :]
        values = jnp.concatenate([values, jnp.ones_like(values)], axis=1)
        results = []
        for head in range(2):
            own = jnp.where(low if head == 0 else ~low, query, jnp.zeros_like(query))
            scores = dot(own, keys, dims=((1,), (1,)))
            top = jnp.max(scores, axis=1, keepdims=True)
            weights = jnp.exp(scores - top).astype(BF16)
            both = dot(weights, values)
            results.append(both[:, :LANES] / both[:, LANES:])
        return jnp.where(low, results[0], results[1]).astype(BF16)

    def step(g, carry):
        @pl.when(g + 3 < WAVES)
        def _():
            kv_start(g + 3)

        @pl.when(g == RING)
        def _():
            b_ring.wait(3)
            o_ring.go(0)

        @pl.when(g == 2)
        def _():
            xb(2)
            xa(3)
            o_ring.go(1)

        @pl.when(g == 3)
        def _():
            o_ring.go(2)

        at_wave = jnp.where(g > RING, g - 1, g)

        @pl.when(g != RING)
        def _():
            xx_wait(at_wave)

        def lay(tile):
            for at in range(NX):
                for t in range(3):
                    w_nat[at * 256 : (at + 1) * 256, t * LANES : (t + 1) * LANES] = tile(at, t)
                rows = dot(part_pick[...], tile(at, 3)).astype(BF16)
                for t in range(3):
                    w_nat[1024 + at * 64 : 1024 + (at + 1) * 64, t * LANES : (t + 1) * LANES] = rows[
                        t * 64 : (t + 1) * 64
                    ]

        @pl.when(g != RING)
        def _():
            lay(lambda at, t: w_buf[at_wave, at, :, :, t].reshape(256, LANES))

        @pl.when(g == RING)
        def _():
            lay(lambda at, t: b_buf[:, at, :, t].reshape(256, LANES))

        result = dot(nrm[...], w_nat[...])
        qb[...] = (result[:, :LANES] * 0.125).astype(BF16)
        for t in range(2):
            new = result[:, (t + 1) * LANES : (t + 2) * LANES].astype(BF16)
            kvb[g, t, block(1)] = new[:TOK]
            kvb[g, t, block(4)] = new[TOK:]
        fkv_own(g).start()
        fkv_copy(g).start()
        kv_wait(g)

        @pl.when(g == WAVES - 1)
        def _():
            o_ring.wait(3)
            for at in range(NX):
                heads = [o_buf[:, at, :, i].reshape(256, LANES) for i in range(WAVES)]
                rest = [
                    b_buf[:, at, :, 3].reshape(256, LANES)
                    if i == RING
                    else w_buf[i - (i > RING), at, :, :, 3].reshape(256, LANES)
                    for i in range(WAVES)
                ]
                stack = jnp.concatenate([jnp.concatenate(heads, axis=1), jnp.concatenate(rest, axis=1)], axis=0)
                wo_nat[core, at * 320 : (at + 1) * 320, :] = dot(picks[...], stack).astype(BF16)
            won_copy().start()

        ho_out[g] = attend(g, 1)
        ho_copy(g).start()

        @pl.when(g == 0)
        def _():
            xb(1)
            zb(3)
            xa(2)

        @pl.when(g == 3)
        def _():
            xb(3)
            o_ring.go(3)

        ho[core * WAVES + g] = attend(g, 0)
        return carry

    lax.fori_loop(0, WAVES, step, 0)

    for g in range(WAVES):
        ho_wait(g)
    there = wo_nat.at[1 - core]
    remote(there, there, won_s, won_r, sib).wait_recv()
    lhs = jnp.concatenate([ho[i] for i in range(2 * WAVES)], axis=1)
    for i in range(2):
        att_ref[:, i * HALF : (i + 1) * HALF] = dot(lhs, wo_nat[i]).astype(BF16)

    for copy in mom_copies() + y_copies() + [nrm_copy(), won_copy()]:
        copy.wait_send()
    b_ring.drain()
    o_ring.drain()

    def drain_direct(g, carry):
        for copy in z_copies(g) + zz_copies(g) + x_copies(g) + xx_copies(g):
            copy.wait_send()
        return carry

    lax.fori_loop(0, DIRECT, drain_direct, 0)

    def drain(g, carry):
        for copy in kv_copies(g) + [fkv_copy(g), ho_copy(g)]:
            copy.wait_send()
        fkv_wait(g)
        fkv_own(g).wait()
        return carry

    lax.fori_loop(0, WAVES, drain, 0)


def shards(tokens, stale_kv, stale_moments, norm_gain, norm_bias, w_query, w_key, w_value, w_out):
    vmem = pl.BlockSpec(memory_space=pltpu.VMEM)
    hbm = pl.BlockSpec(memory_space=pl.ANY)
    dma = pltpu.SemaphoreType.DMA
    attended, fresh_kv, sums, squares = pl.pallas_call(
        kernel,
        out_shape=(
            jax.ShapeDtypeStruct((TOK, CH), BF16),
            jax.ShapeDtypeStruct((2, TOK, CH), BF16),
            jax.ShapeDtypeStruct((1, GROUPS), F32),
            jax.ShapeDtypeStruct((1, GROUPS), F32),
        ),
        in_specs=[vmem, hbm] + [vmem] * 7,
        out_specs=(vmem, hbm, vmem, vmem),
        scratch_shapes=[
            pltpu.VMEM((DIRECT, NX, NZ, NY, 4, 16, LANES), BF16),
            pltpu.VMEM((NZ, NX, NY, 4, 16, LANES), BF16),
            pltpu.VMEM((NZ, NX, NY, WAVES, 16, LANES), BF16),
            pltpu.VMEM((CH, 3 * LANES), BF16),
            pltpu.VMEM((2, CH, HALF), BF16),
            pltpu.VMEM((320, 512), BF16),
            pltpu.VMEM((192, 256), BF16),
            pltpu.VMEM((HALF, HALF), BF16),
            pltpu.VMEM((16, HALF), F32),
            pltpu.VMEM((WAVES, 2, 6 * TOK, LANES), BF16),
            pltpu.VMEM((2 * TOK, CH), BF16),
            pltpu.VMEM((2 * TOK, LANES), BF16),
            pltpu.VMEM((2 * WAVES, TOK, LANES), BF16),
            pltpu.VMEM((WAVES, TOK, LANES), BF16),
            pltpu.VMEM((4, 8, LANES), F32),
            dma((4,)), dma((4,)),
            dma((DIRECT, 8)), dma((DIRECT, 8)),
            dma((DIRECT, 2)), dma((DIRECT, 2)),
            dma((DIRECT, 2)), dma((DIRECT, 2)),
            dma((3,)), dma((3,)),
            dma((8,)), dma((8,)),
            dma((3,)), dma((3,)),
            dma((8,)), dma((8,)),
            dma((WAVES, 3)), dma((WAVES, 3)), dma((WAVES,)),
            dma((3,)), dma((3,)),
            dma, dma,
            dma((WAVES,)), dma((WAVES,)), dma((WAVES,)),
            dma((WAVES,)), dma((WAVES,)),
            dma, dma,
        ],
        compiler_params=pltpu.CompilerParams(
            collective_id=0, has_side_effects=True, vmem_limit_bytes=60 << 20
        ),
        name="block",
    )(
        tokens.reshape(TOK, CH), stale_kv[0], stale_moments[0, 0],
        norm_gain, norm_bias, w_query, w_key, w_value, w_out,
    )
    return (
        attended.reshape(tokens.shape),
        fresh_kv[None],
        sums[None],
        squares[None],
    )


def solution(mesh):
    in_specs = (
        P("rows", None, "strips", None),
        P("rows", None, "strips", None),
        P("rows", "strips", None, None),
        P(),
        P(),
        P("rows", None),
        P("rows", None),
        P("rows", None),
        P("rows", None),
    )
    out_specs = (
        P("rows", None, "strips", None),
        P("rows", None, "strips", None),
        P("rows", "strips", None),
        P("rows", "strips", None),
    )
    return jax.shard_map(shards, mesh=mesh, in_specs=in_specs, out_specs=out_specs, check_vma=False)
```

```python
import jax
import jax.numpy as jnp
from jax import lax
from jax.experimental import pallas as pl
from jax.experimental.pallas import tpu as pltpu
from jax.sharding import PartitionSpec as P

MESH = pl.DeviceIdType.MESH
F32 = jnp.float32
BF16 = jnp.bfloat16

TOK = 384
CH = 1280
HALF = 640
LANES = 128
WAVES = 5
RING = 1
DIRECT = WAVES - 1
NX, NZ, NY = 4, 8, 2
SHARD = 20
GROUPS = 32
PER_GROUP = 40


def dot(a, b, dims=((1,), (0,)), precision=None):
    return lax.dot_general(a, b, (dims, ((), ())), precision=precision, preferred_element_type=F32)


def kernel(
    tok_ref, kv_ref, mom_ref, gain_ref, bias_ref, wq_ref, wk_ref, wv_ref, wo_ref,
    att_ref, fkv_ref, fs_ref, fq_ref,
    w_buf, b_buf, o_buf, w_nat, wo_nat, picks, part_pick, order, tail, kvb, nrm, qb, ho, ho_out, moms,
    y_s, y_r, z_s, z_r, x_s, x_r, xx_s, xx_r, bx_s, bx_r, bz_s, bz_r, ox_s, ox_r, oz_s, oz_r,
    kv_s, kv_r, kv_l, mom_s, mom_r, nrm_s, nrm_r, fkv_s, fkv_r, fkv_l, ho_s, ho_r, won_s, won_r,
):
    row = lax.axis_index("rows")
    strip = lax.axis_index("strips")
    ylo = row % 2
    z = (row // 2) % NZ
    x = row // (2 * NZ)
    core = strip % 2
    yhi = strip // 2

    sib = (row, yhi * 2 + 1 - core)
    far = (row, (1 - yhi) * 2 + core)
    far_other = (row, (1 - yhi) * 2 + 1 - core)
    y_peer = (x * 16 + z * 2 + 1 - ylo, strip)

    def z_at(d):
        return (z + NZ + d) % NZ

    def z_peer(d):
        return (x * 16 + z_at(d) * 2 + ylo, strip)

    xl = (x + NX - 1) % NX
    xr = (x + 1) % NX
    x_far = (x + 2) % NX
    x_left = (xl * 16 + z * 2 + ylo, strip)
    x_right = (xr * 16 + z * 2 + ylo, strip)
    x_across = (x_far * 16 + z * 2 + ylo, strip)

    barrier = pltpu.get_barrier_semaphore()
    everyone = [sib, far, far_other, y_peer, x_left, x_right, x_across] + [z_peer(d) for d in (1, -1, 2, -2)]
    for peer in everyone:
        pl.semaphore_signal(barrier, inc=1, device_id=peer, device_id_type=MESH)

    def remote(src, dst, send, recv, to):
        return pltpu.make_async_remote_copy(
            src_ref=src, dst_ref=dst, send_sem=send, recv_sem=recv, device_id=to, device_id_type=MESH
        )

    mine = pl.ds(pl.multiple_of(core * HALF, LANES), HALF)
    for t, ref in enumerate((wq_ref, wk_ref, wv_ref, wo_ref)):
        rows = ref[:, mine]
        for g in range(WAVES):
            piece = rows[:16, g * LANES : (g + 1) * LANES]
            if t == 3:
                o_buf[z, x, ylo, g] = piece
            elif g == RING:
                b_buf[z, x, ylo, t] = piece
            else:
                w_buf[g - (g > RING), x, z, ylo, t] = piece
        tail[4 * t : 4 * t + 4, :] = rows.astype(F32)[16:SHARD, :]
    rest = tail[...].astype(BF16)
    for g in range(WAVES):
        piece = rest[:, g * LANES : (g + 1) * LANES]
        if g == RING:
            b_buf[z, x, ylo, 3] = piece
        else:
            w_buf[g - (g > RING), x, z, ylo, 3] = piece
    moms[0] = jnp.zeros((8, LANES), F32)
    moms[0, 0:2, 0:GROUPS] = mom_ref[...]

    pl.semaphore_wait(barrier, len(everyone))

    def y_refs(side):
        return (
            w_buf.at[0, x, z, side],
            b_buf.at[z, x, side],
            w_buf.at[pl.ds(1, DIRECT - 1), x, z, side],
            o_buf.at[z, x, side],
        )

    def y_copies():
        return [remote(ref, ref, y_s.at[i], y_r.at[i], y_peer) for i, ref in enumerate(y_refs(ylo))]

    def y_wait(i):
        there = y_refs(1 - ylo)[i]
        remote(there, there, y_s.at[i], y_r.at[i], y_peer).wait_recv()

    def z_copies(g):
        here = w_buf.at[g, x, z]
        return [
            remote(here, here, z_s.at[g, i], z_r.at[g, i], z_peer(d)) for i, d in enumerate((1, -1, 2, -2))
        ]

    def zz_copies(g):
        left, right = w_buf.at[g, x, z_at(-2)], w_buf.at[g, x, z_at(2)]
        left_half, right_half = w_buf.at[g, x, z_at(-2), 0], w_buf.at[g, x, z_at(2), 1]
        return [
            remote(ref, ref, z_s.at[g, i + 4], z_r.at[g, i + 4], z_peer(d))
            for i, (ref, d) in enumerate(((left, 1), (right, -1), (left_half, 2), (right_half, -2)))
        ]

    def z_wait(g, which):
        for i in which:
            there = w_buf.at[g, x, z_at((-1, 1, -2, 2, -3, 3)[i])] if i < 6 else w_buf.at[g, x, z_at(4), i - 6]
            remote(there, there, z_s.at[g, i], z_r.at[g, i], x_right).wait_recv()

    class Ring:
        def __init__(self, buf, x_send, x_recv, send, recv):
            self.buf, self.x_send, self.x_recv, self.send, self.recv = buf, x_send, x_recv, send, recv

        def x_copies(self):
            here = self.buf.at[z, x]
            return [
                remote(here, here, self.x_send.at[i], self.x_recv.at[i], to)
                for i, to in enumerate((x_right, x_across, x_left))
            ]

        def x_wait(self):
            for i, at in enumerate((xl, x_far, xr)):
                there = self.buf.at[z, at]
                remote(there, there, self.x_send.at[i], self.x_recv.at[i], x_right).wait_recv()

        def refs(self, step):
            if step < 3:
                return self.buf.at[z_at(-1 - step)], self.buf.at[z_at(1 + step)]
            return self.buf.at[z_at(4), pl.ds(0, 2)], self.buf.at[z_at(4), pl.ds(2, 2)]

        def copies(self, step):
            if step == 0:
                refs = self.buf.at[z], self.buf.at[z]
            elif step < 3:
                refs = self.refs(step - 1)
            else:
                refs = self.buf.at[z_at(-3), pl.ds(0, 2)], self.buf.at[z_at(3), pl.ds(2, 2)]
            return [
                remote(ref, ref, self.send.at[2 * step + i], self.recv.at[2 * step + i], z_peer(d))
                for i, (ref, d) in enumerate(zip(refs, (1, -1)))
            ]

        def wait(self, step):
            for i, there in enumerate(self.refs(step)):
                remote(there, there, self.send.at[2 * step + i], self.recv.at[2 * step + i], x_right).wait_recv()

        def go(self, step):
            if step == 0:
                self.x_wait()
            else:
                self.wait(step - 1)
            start(self.copies(step))

        def drain(self):
            for copy in self.x_copies() + [c for step in range(4) for c in self.copies(step)]:
                copy.wait_send()

    b_ring = Ring(b_buf, bx_s, bx_r, bz_s, bz_r)
    o_ring = Ring(o_buf, ox_s, ox_r, oz_s, oz_r)

    def x_copies(g):
        here = w_buf.at[g, x]
        return [
            remote(here, here, x_s.at[g, 0], x_r.at[g, 0], x_right),
            remote(here, here, x_s.at[g, 1], x_r.at[g, 1], x_left),
        ]

    def x_wait(g):
        for i, at in ((0, xl), (1, xr)):
            there = w_buf.at[g, at]
            remote(there, there, x_s.at[g, i], x_r.at[g, i], x_right).wait_recv()

    def xx_copies(g):
        first, second = w_buf.at[g, xl, pl.ds(0, NZ // 2)], w_buf.at[g, xr, pl.ds(NZ // 2, NZ // 2)]
        return [
            remote(first, first, xx_s.at[g, 0], xx_r.at[g, 0], x_right),
            remote(second, second, xx_s.at[g, 1], xx_r.at[g, 1], x_left),
        ]

    def xx_wait(g):
        for i in (0, 1):
            there = w_buf.at[g, x_far, pl.ds(i * (NZ // 2), NZ // 2)]
            remote(there, there, xx_s.at[g, i], xx_r.at[g, i], x_right).wait_recv()

    def lanes(which, g):
        return pl.ds(pl.multiple_of(which * HALF + g * LANES, LANES), LANES)

    def block(i):
        return pl.ds(i * TOK, TOK)

    def kv_copies(g):
        mine_g, other_g = kv_ref.at[:, :, lanes(core, g)], kv_ref.at[:, :, lanes(1 - core, g)]
        return [
            remote(other_g, kvb.at[g, :, block(0)], kv_s.at[g, 0], kv_r.at[g, 0], sib),
            remote(mine_g, kvb.at[g, :, block(2)], kv_s.at[g, 1], kv_r.at[g, 1], far),
            remote(other_g, kvb.at[g, :, block(3)], kv_s.at[g, 2], kv_r.at[g, 2], far_other),
        ]

    def kv_own(g):
        return pltpu.make_async_copy(kv_ref.at[:, :, lanes(core, g)], kvb.at[g, :, block(5)], kv_l.at[g])

    def kv_wait(g):
        for i, b in enumerate((0, 2, 3)):
            there = kvb.at[g, :, block(b)]
            remote(there, there, kv_s.at[g, i], kv_r.at[g, i], sib).wait_recv()
        kv_own(g).wait()

    def mom_copies():
        return [
            remote(moms.at[0], moms.at[i + 1], mom_s.at[i], mom_r.at[i], to)
            for i, to in enumerate((sib, far, far_other))
        ]

    def nrm_copy():
        return remote(nrm.at[pl.ds(0, TOK)], nrm.at[pl.ds(TOK, TOK)], nrm_s, nrm_r, sib)

    def fkv_copy(g):
        return remote(kvb.at[g, :, block(4)], fkv_ref.at[:, :, lanes(core, g)], fkv_s.at[g], fkv_r.at[g], sib)

    def fkv_own(g):
        return pltpu.make_async_copy(kvb.at[g, :, block(1)], fkv_ref.at[:, :, lanes(core, g)], fkv_l.at[g])

    def fkv_wait(g):
        there = fkv_ref.at[:, :, lanes(1 - core, g)]
        remote(there, there, fkv_s.at[g], fkv_r.at[g], sib).wait_recv()

    def ho_copy(g):
        return remote(ho_out.at[g], ho.at[core * WAVES + g], ho_s.at[g], ho_r.at[g], sib)

    def ho_wait(g):
        there = ho.at[(1 - core) * WAVES + g]
        remote(there, there, ho_s.at[g], ho_r.at[g], sib).wait_recv()

    def won_copy():
        return remote(wo_nat.at[core], wo_nat.at[core], won_s, won_r, sib)

    def start(copies):
        for copy in copies:
            copy.start()

    def kv_start(g):
        start(kv_copies(g))
        kv_own(g).start()

    def za(g):
        start(z_copies(g))

    def zb(g):
        z_wait(g, (2, 3))
        start(zz_copies(g))

    def xa(g):
        z_wait(g, (0, 1, 4, 5, 6, 7))
        start(x_copies(g))

    def xb(g):
        x_wait(g)
        start(xx_copies(g))

    start(y_copies())
    start(mom_copies())
    kv_start(0)

    channel = lax.broadcasted_iota(jnp.int32, (CH, LANES), 0)
    group = lax.broadcasted_iota(jnp.int32, (CH, LANES), 1)
    member = jnp.where((channel >= group * PER_GROUP) & (channel < (group + 1) * PER_GROUP), 1.0, 0.0)
    toks = tok_ref[...].astype(F32)
    sums = jnp.sum(toks, axis=0, keepdims=True)
    squares = jnp.sum(toks * toks, axis=0, keepdims=True)
    pick = lax.broadcasted_iota(jnp.int32, (8, CH), 0)
    stacked = jnp.where(pick == 0, sums, jnp.where(pick == 1, squares, 0.0))
    fresh = dot(stacked, member, precision=lax.Precision.HIGHEST)
    fs_ref[...] = fresh[0:1, 0:GROUPS]
    fq_ref[...] = fresh[1:2, 0:GROUPS]

    y_wait(0)
    za(0)
    y_wait(1)
    start(b_ring.x_copies())
    kv_start(1)
    kv_start(2)

    k_at = lax.broadcasted_iota(jnp.int32, (HALF, HALF), 0)
    j_at = lax.broadcasted_iota(jnp.int32, (HALF, HALF), 1)
    first = (j_at >> 8) * 320 + ((j_at & 255) >> 4) * SHARD + (j_at & 15)
    j_at = j_at - 512
    last = (j_at >> 6) * 320 + ((j_at & 63) >> 2) * SHARD + 16 + (j_at & 3)
    order[...] = jnp.where(k_at == jnp.where(j_at < 0, first, last), 1.0, 0.0).astype(BF16)
    r_at = lax.broadcasted_iota(jnp.int32, (192, 256), 0)
    j_at = lax.broadcasted_iota(jnp.int32, (192, 256), 1)
    hit = j_at == ((r_at & 63) >> 2) * 16 + (r_at >> 6) * 4 + (r_at & 3)
    part_pick[...] = jnp.where(hit, 1.0, 0.0).astype(BF16)

    zb(0)
    b_ring.go(0)

    for i in range(3):
        there = moms.at[i + 1]
        remote(there, there, mom_s.at[i], mom_r.at[i], sib).wait_recv()
    mixed = (moms[1] + moms[2] + moms[3]) + fresh
    count = float(TOK * 4 * PER_GROUP)
    mean = mixed[0:1, :] / count
    var = mixed[1:2, :] / count - mean * mean
    rstd = lax.rsqrt(var + 1e-05)
    pick = lax.broadcasted_iota(jnp.int32, (8, LANES), 0)
    inside = lax.broadcasted_iota(jnp.int32, (8, LANES), 1) < GROUPS
    stats = jnp.where(inside, jnp.where(pick == 0, mean, jnp.where(pick == 1, rstd, 0.0)), 0.0)
    spread = dot(stats, member, dims=((1,), (1,)), precision=lax.Precision.HIGHEST)
    normed = (tok_ref[...].astype(F32) - spread[0:1, :]) * spread[1:2, :]
    normed = (normed * gain_ref[...][None] + bias_ref[...][None]).astype(BF16)
    for i in range(2):
        moved = dot(normed[:, i * HALF : (i + 1) * HALF], order[...]).astype(BF16)
        nrm[0:TOK, i * 512 : (i + 1) * 512] = moved[:, :512]
        nrm[0:TOK, 1024 + i * LANES : 1024 + (i + 1) * LANES] = moved[:, 512:]
    nrm_copy().start()

    xa(0)
    y_wait(2)
    y_wait(3)
    za(1)
    b_ring.go(1)
    k_at = lax.broadcasted_iota(jnp.int32, (320, 256), 0)
    j_at = lax.broadcasted_iota(jnp.int32, (320, 256), 1)
    base = (j_at >> 4) * SHARD
    picks[:, :256] = jnp.where(k_at == base + (j_at & 15), 1.0, 0.0).astype(BF16)
    hit = (k_at == base + 16 + (j_at & 3)) & (((j_at >> 2) & 3) == 3)
    picks[:, 256:] = jnp.where(hit, 1.0, 0.0).astype(BF16)
    zb(1)
    za(2)
    b_ring.go(2)
    xb(0)
    xa(1)
    zb(2)
    b_ring.go(3)
    za(3)
    start(o_ring.x_copies())
    there = nrm.at[pl.ds(TOK, TOK)]
    remote(there, there, nrm_s, nrm_r, sib).wait_recv()

    low = lax.broadcasted_iota(jnp.int32, (TOK, LANES), 1) < LANES // 2

    def attend(g, which):
        query = qb[pl.ds(which * TOK, TOK), :]
        keys = kvb[g, 0, pl.ds(which * 2 * TOK, 4 * TOK), :]
        values = kvb[g, 1, pl.ds(which * 2 * TOK, 4 * TOK), :]
        values = jnp.concatenate([values, jnp.ones_like(values)], axis=1)
        results = []
        for head in range(2):
            own = jnp.where(low if head == 0 else ~low, query, jnp.zeros_like(query))
            scores = dot(own, keys, dims=((1,), (1,)))
            top = jnp.max(scores, axis=1, keepdims=True)
            weights = jnp.exp(scores - top).astype(BF16)
            both = dot(weights, values)
            results.append(both[:, :LANES] / both[:, LANES:])
        return jnp.where(low, results[0], results[1]).astype(BF16)

    def step(g, carry):
        @pl.when(g + 3 < WAVES)
        def _():
            kv_start(g + 3)

        @pl.when(g == RING)
        def _():
            b_ring.wait(3)
            o_ring.go(0)

        @pl.when(g == 2)
        def _():
            xb(2)
            xa(3)
            o_ring.go(1)

        @pl.when(g == 3)
        def _():
            o_ring.go(2)

        at_wave = jnp.where(g > RING, g - 1, g)

        @pl.when(g != RING)
        def _():
            xx_wait(at_wave)

        def lay(tile):
            for at in range(NX):
                for t in range(3):
                    w_nat[at * 256 : (at + 1) * 256, t * LANES : (t + 1) * LANES] = tile(at, t)
                rows = dot(part_pick[...], tile(at, 3)).astype(BF16)
                for t in range(3):
                    w_nat[1024 + at * 64 : 1024 + (at + 1) * 64, t * LANES : (t + 1) * LANES] = rows[
                        t * 64 : (t + 1) * 64
                    ]

        @pl.when(g != RING)
        def _():
            lay(lambda at, t: w_buf[at_wave, at, :, :, t].reshape(256, LANES))

        @pl.when(g == RING)
        def _():
            lay(lambda at, t: b_buf[:, at, :, t].reshape(256, LANES))

        result = dot(nrm[...], w_nat[...])
        qb[...] = (result[:, :LANES] * 0.125).astype(BF16)
        for t in range(2):
            new = result[:, (t + 1) * LANES : (t + 2) * LANES].astype(BF16)
            kvb[g, t, block(1)] = new[:TOK]
            kvb[g, t, block(4)] = new[TOK:]
        fkv_own(g).start()
        fkv_copy(g).start()
        kv_wait(g)

        @pl.when(g == WAVES - 1)
        def _():
            o_ring.wait(3)
            for at in range(NX):
                heads = [o_buf[:, at, :, i].reshape(256, LANES) for i in range(WAVES)]
                rest = [
                    b_buf[:, at, :, 3].reshape(256, LANES)
                    if i == RING
                    else w_buf[i - (i > RING), at, :, :, 3].reshape(256, LANES)
                    for i in range(WAVES)
                ]
                stack = jnp.concatenate([jnp.concatenate(heads, axis=1), jnp.concatenate(rest, axis=1)], axis=0)
                wo_nat[core, at * 320 : (at + 1) * 320, :] = dot(picks[...], stack).astype(BF16)
            won_copy().start()

        ho_out[g] = attend(g, 1)
        ho_copy(g).start()

        @pl.when(g == 0)
        def _():
            xb(1)
            zb(3)
            xa(2)

        @pl.when(g == 3)
        def _():
            xb(3)
            o_ring.go(3)

        ho[core * WAVES + g] = attend(g, 0)
        return carry

    lax.fori_loop(0, WAVES, step, 0)

    for g in range(WAVES):
        ho_wait(g)
    there = wo_nat.at[1 - core]
    remote(there, there, won_s, won_r, sib).wait_recv()
    lhs = jnp.concatenate([ho[i] for i in range(2 * WAVES)], axis=1)
    for i in range(2):
        att_ref[:, i * HALF : (i + 1) * HALF] = dot(lhs, wo_nat[i]).astype(BF16)

    for copy in mom_copies() + y_copies() + [nrm_copy(), won_copy()]:
        copy.wait_send()
    b_ring.drain()
    o_ring.drain()

    def drain_direct(g, carry):
        for copy in z_copies(g) + zz_copies(g) + x_copies(g) + xx_copies(g):
            copy.wait_send()
        return carry

    lax.fori_loop(0, DIRECT, drain_direct, 0)

    def drain(g, carry):
        for copy in kv_copies(g) + [fkv_copy(g), ho_copy(g)]:
            copy.wait_send()
        fkv_wait(g)
        fkv_own(g).wait()
        return carry

    lax.fori_loop(0, WAVES, drain, 0)


def shards(tokens, stale_kv, stale_moments, norm_gain, norm_bias, w_query, w_key, w_value, w_out):
    vmem = pl.BlockSpec(memory_space=pltpu.VMEM)
    hbm = pl.BlockSpec(memory_space=pl.ANY)
    dma = pltpu.SemaphoreType.DMA
    attended, fresh_kv, sums, squares = pl.pallas_call(
        kernel,
        out_shape=(
            pltpu.VMEM((TOK, CH), BF16),
            pltpu.VMEM((2, TOK, CH), BF16),
            jax.ShapeDtypeStruct((1, GROUPS), F32),
            jax.ShapeDtypeStruct((1, GROUPS), F32),
        ),
        in_specs=[vmem, hbm] + [vmem] * 7,
        out_specs=(vmem, vmem, vmem, vmem),
        scratch_shapes=[
            pltpu.VMEM((DIRECT, NX, NZ, NY, 4, 16, LANES), BF16),
            pltpu.VMEM((NZ, NX, NY, 4, 16, LANES), BF16),
            pltpu.VMEM((NZ, NX, NY, WAVES, 16, LANES), BF16),
            pltpu.VMEM((CH, 3 * LANES), BF16),
            pltpu.VMEM((2, CH, HALF), BF16),
            pltpu.VMEM((320, 512), BF16),
            pltpu.VMEM((192, 256), BF16),
            pltpu.VMEM((HALF, HALF), BF16),
            pltpu.VMEM((16, HALF), F32),
            pltpu.VMEM((WAVES, 2, 6 * TOK, LANES), BF16),
            pltpu.VMEM((2 * TOK, CH), BF16),
            pltpu.VMEM((2 * TOK, LANES), BF16),
            pltpu.VMEM((2 * WAVES, TOK, LANES), BF16),
            pltpu.VMEM((WAVES, TOK, LANES), BF16),
            pltpu.VMEM((4, 8, LANES), F32),
            dma((4,)), dma((4,)),
            dma((DIRECT, 8)), dma((DIRECT, 8)),
            dma((DIRECT, 2)), dma((DIRECT, 2)),
            dma((DIRECT, 2)), dma((DIRECT, 2)),
            dma((3,)), dma((3,)),
            dma((8,)), dma((8,)),
            dma((3,)), dma((3,)),
            dma((8,)), dma((8,)),
            dma((WAVES, 3)), dma((WAVES, 3)), dma((WAVES,)),
            dma((3,)), dma((3,)),
            dma, dma,
            dma((WAVES,)), dma((WAVES,)), dma((WAVES,)),
            dma((WAVES,)), dma((WAVES,)),
            dma, dma,
        ],
        compiler_params=pltpu.CompilerParams(
            collective_id=0, has_side_effects=True, vmem_limit_bytes=60 << 20
        ),
        name="block",
    )(
        tokens.reshape(TOK, CH), stale_kv[0], stale_moments[0, 0],
        norm_gain, norm_bias, w_query, w_key, w_value, w_out,
    )
    return (
        attended.reshape(tokens.shape),
        fresh_kv[None],
        sums[None],
        squares[None],
    )


def solution(mesh):
    in_specs = (
        P("rows", None, "strips", None),
        P("rows", None, "strips", None),
        P("rows", "strips", None, None),
        P(),
        P(),
        P("rows", None),
        P("rows", None),
        P("rows", None),
        P("rows", None),
    )
    out_specs = (
        P("rows", None, "strips", None),
        P("rows", None, "strips", None),
        P("rows", "strips", None),
        P("rows", "strips", None),
    )
    return jax.shard_map(shards, mesh=mesh, in_specs=in_specs, out_specs=out_specs, check_vma=False)
```
